256 devices in a mesh: cells: 128 (over z, x, y), genes: 2 (over core).
Axes of the slice: x: 4, y: 4, z: 8, core: 2. Of those that a mesh axis runs over, the one named last changes fastest.
Arguments:
- stored: bfloat16 [256, 2, 65536], P('cells', 'genes'), may hold values from 0.001 to 70, as said below
- neighbours: int32 [512, 8], P('cells'), may hold values from 0 to 511, as said below
- counts: int32 [512], P('cells'), may hold values from 5 to 8
- affinity: bfloat16 [512, 8, 128, 128], P('cells'), may hold values from 9.9658966e-05 to 1
Outputs:
- imputed: float32 [512, 65536], P('genes', 'cells')
The draws below stay inside these ranges and needn't reach their ends.
Inputs may be any that keep to these rules, and one draw needn't show every extreme that they name: `stored`: entries are positive. neighbours[b, 0] = b. Slots 1 to 4 of every row block name blocks of other devices along cells (block j lies on device j // 4); slots 5 to 7 name blocks of the row block's own device. Over the row blocks of one device, slots 1 to 4 name blocks of any one other device at most 1 times, and exactly 1 times for some device.
All inputs are finite; a program needn't handle non-finite values.
Results may differ from the reference program's by a relative error of at most 0.007.
Values may be sent and summed in bfloat16 or wider, within the bound.
No kernel may reach another device: no remote copies, remote signals or barrier semaphores. Data moves between devices by JAX's collectives and lax.ppermute only.
A program may use at most 64 MiB of HBM per device.

```python
import math
import jax
import jax.numpy as jnp
from jax import lax

GENES = 512
BS = 128
SLOTS = 8
REMOTE = 4
STEPS = 3
BLK_DEV = 4
BLOCKS = 512
CELLS = 65536
GCHUNK = 256


def draw_stored(key, part):
    key = jax.random.fold_in(key, 11)
    key_cell, key_prog, key_noise = jax.random.split(key, 3)
    halves = GENES // GCHUNK
    full_shape = (GCHUNK, halves, CELLS)
    cell_scale = jnp.exp(jax.random.uniform(key_cell, (1, 1, CELLS), jnp.float32, math.log(0.3), math.log(3.0)))
    program = jnp.exp(jax.random.uniform(key_prog, (GCHUNK, halves, BLOCKS, 1), jnp.float32, math.log(0.1), 0.0))
    noise = jnp.exp(0.4 * jnp.clip(jax.random.normal(key_noise, full_shape, jnp.float32), -4.0, 4.0))
    half_scale = 1.0 + 2.0 * jnp.arange(halves, dtype=jnp.float32)
    program = jnp.broadcast_to(program, (GCHUNK, halves, BLOCKS, BS)).reshape(GCHUNK, halves, CELLS)
    values = cell_scale * program * noise * half_scale[None, :, None]
    return values.astype(jnp.bfloat16)


def draw_neighbours(key, part):
    key = jax.random.fold_in(key, 23)
    key_order, key_far, key_near, key_peer = jax.random.split(key, 4)
    device_total = BLOCKS // BLK_DEV
    remote_total = REMOTE * BLK_DEV
    orders = jax.vmap(lambda one_key: jax.random.permutation(one_key, remote_total))(jax.random.split(key_order, device_total))
    peer_orders = jax.vmap(lambda one_key: jax.random.permutation(one_key, device_total - 1))(jax.random.split(key_peer, device_total))
    picked = jnp.take_along_axis(peer_orders.astype(jnp.int32), orders.astype(jnp.int32) % (device_total - 1), axis=1)
    device_ids = jnp.arange(device_total, dtype=jnp.int32)[:, None]
    peer_dev = (device_ids + 1 + picked) % device_total
    far_ids = peer_dev * BLK_DEV + jax.random.randint(key_far, (device_total, remote_total), 0, BLK_DEV, jnp.int32)
    far_ids = far_ids.reshape(BLOCKS, REMOTE)
    own_ids = jnp.arange(BLOCKS, dtype=jnp.int32)
    home_base = own_ids // BLK_DEV * BLK_DEV
    near_ids = home_base[:, None] + jax.random.randint(key_near, (BLOCKS, SLOTS - 1 - REMOTE), 0, BLK_DEV, jnp.int32)
    return jnp.concatenate([own_ids[:, None], far_ids, near_ids], axis=1).astype(jnp.int32)


def place_ends(values, stream_key, low, largest):
    longest = values.shape.index(max(values.shape))
    spots = []
    for shift in (0, 1):
        where = [jax.random.randint(jax.random.fold_in(stream_key, axis), (), 0, length) for axis, length in enumerate(values.shape)]
        where[longest] = (where[longest] + shift) % values.shape[longest]
        spots.append(tuple(where))
    return values.at[spots[0]].set(low).at[spots[1]].set(largest)


def levels(key, dims, shards, least, high):
    factor_of = 1.0
    for axis_at, parts in shards:
        draws = jax.random.uniform(jax.random.fold_in(jax.random.fold_in(key, 6), axis_at), (parts,), jnp.float32, least / len(shards), high / len(shards))
        factor_of = factor_of * jnp.repeat(jnp.exp(draws), dims[axis_at] // parts).reshape((-1,) + (1,) * (len(dims) - 1 - axis_at))
    return factor_of


def setup_inputs(seed: int = 0) -> dict:
    arg_keys = jax.random.split(jax.random.key(seed), 5)
    stored = draw_stored(jax.random.fold_in(arg_keys[4], 71), 0)
    neighbours = draw_neighbours(jax.random.fold_in(arg_keys[4], 71), 0)
    counts = place_ends(jax.random.randint(arg_keys[2], (BLOCKS,), REMOTE + 1, SLOTS + 1), jax.random.fold_in(arg_keys[2], 1), REMOTE + 1, SLOTS).astype(jnp.int32)
    affinity = jnp.clip(jnp.exp(math.log(1.0) - 9.213757 * jax.random.uniform(arg_keys[3], (BLOCKS, SLOTS, BS, BS), jnp.float32) ** levels(arg_keys[3], (BLOCKS, SLOTS, BS, BS), ((0, 128),), -0.2, 0.2)), 9.965896606445312e-05, 1.0).astype(jnp.bfloat16)
    return dict(stored=stored, neighbours=neighbours, counts=counts, affinity=affinity)


epsilon = 1e-6


def reference(stored, neighbours, counts, affinity):
    expression = jnp.transpose(stored, (1, 0, 2)).reshape(GENES, CELLS).astype(jnp.float32)
    library = jnp.sum(expression, axis=0) / GENES
    current = (expression / library[None, :]).astype(jnp.bfloat16)
    current = jnp.transpose(current.reshape(GENES, BLOCKS, BS), (1, 0, 2))
    peak_first = jnp.max(current, axis=(0, 2)).astype(jnp.float32)
    scaled = current.astype(jnp.float32)
    for step_index in range(STEPS):
        def one_block(block_items, source=current):
            neighbour_ids, live_count, tile_rows, own_rows = block_items
            valid_mask = (jnp.arange(SLOTS) < live_count).astype(jnp.float32)
            masked = tile_rows.astype(jnp.float32) * valid_mask[:, None, None]
            rowsum = jnp.sum(masked, axis=(0, 1))
            transition = (masked / rowsum[None, None, :]).astype(jnp.bfloat16)
            operands = source[neighbour_ids].astype(jnp.float32)
            product = jnp.einsum("sgk,ski->gi", operands, transition.astype(jnp.float32))
            return 0.5 * own_rows.astype(jnp.float32) + 0.5 * product

        mixed_sum = lax.map(one_block, (neighbours, counts, affinity, current), batch_size=64)
        peak_now = jnp.max(mixed_sum, axis=(0, 2))
        scaled = mixed_sum * (peak_first / (peak_now + epsilon))[None, :, None]
        current = scaled.astype(jnp.bfloat16)
    return jnp.transpose(scaled, (1, 0, 2)).reshape(GENES, CELLS)
```

```python
import functools

import jax
import jax.numpy as jnp
from jax import lax
from jax.experimental import pallas as pl
from jax.experimental.pallas import tpu as pltpu
from jax.sharding import Mesh, PartitionSpec as P

REMOTE = 4
STEPS = 3
SIDE = 4
GROUP = 8
BS = 128
epsilon = 1e-06
XY = ("x", "y")


def shift(value, axis, distance):
    pairs = [(i, (i + distance) % SIDE) for i in range(SIDE)]
    return lax.ppermute(value, axis, pairs)


def spread(value):
    half = value.shape[0] // 2
    first, second = value[:half], value[half:]
    along_x = [first] + [shift(first, "x", -d) for d in (1, 2, 3)]
    along_y = [second] + [shift(second, "y", -d) for d in (1, 2, 3)]
    first, second = jnp.concatenate(along_x), jnp.concatenate(along_y)
    pieces = [first] + [shift(first, "y", -d) for d in (1, 2, 3)]
    pieces += [second] + [shift(second, "x", -d) for d in (1, 2, 3)]
    return pieces


def step_kernel(pieces, chunk, place_ref, count_ref, *refs):
    sources, (aff_ref, out_ref, peak_ref, own_peak_ref, held, sems) = refs[:pieces], refs[pieces:]
    at = pl.program_id(0)
    size = sources[0].shape[0]

    @pl.when(at == 0)
    def _():
        copies = [
            pltpu.make_async_copy(source, held.at[pl.ds(i * size, size)], sems.at[i])
            for i, source in enumerate(sources)
        ]
        for copy in copies:
            copy.start()
        for copy in copies:
            copy.wait()
        peak_ref[...] = jnp.zeros_like(peak_ref)
        own_peak_ref[...] = jnp.zeros_like(own_peak_ref)

    slots = aff_ref.shape[1]
    genes = held.shape[1]
    peak = peak_ref[...]
    own_peak = own_peak_ref[...]
    for b in range(chunk):
        row = at * chunk + b
        count = count_ref[row]
        tiles = []
        for s in range(slots):
            tile = held[place_ref[row * slots + s]]
            tile = jnp.concatenate([tile, jnp.ones((16, BS), tile.dtype)], axis=0)
            if s > REMOTE:
                tile = jnp.where(s < count, tile, jnp.zeros_like(tile))
            tiles.append(tile)
        left = jnp.concatenate(tiles, axis=1)
        right = aff_ref[b].reshape(slots * BS, BS)
        total = jnp.dot(left, right, preferred_element_type=jnp.float32)
        own = held[place_ref[row * slots]].astype(jnp.float32)
        mixed = 0.5 * own + total[:genes] * (0.5 / total[genes : genes + 1])
        out_ref[b] = mixed.astype(out_ref.dtype)
        peak = jnp.maximum(peak, mixed)
        own_peak = jnp.maximum(own_peak, own)
    peak_ref[...] = peak
    own_peak_ref[...] = own_peak


def diffuse(pieces, places, counts, affinity, out_type):
    blocks, slots = affinity.shape[:2]
    size, genes = pieces[0].shape[:2]
    chunk = 8
    n = len(pieces)
    whole = lambda at, *_: (0, 0)
    return pl.pallas_call(
        functools.partial(step_kernel, n, chunk),
        grid_spec=pltpu.PrefetchScalarGridSpec(
            num_scalar_prefetch=2,
            grid=(blocks // chunk,),
            in_specs=[pl.BlockSpec(memory_space=pl.ANY)] * n
            + [pl.BlockSpec((chunk, slots, BS, BS), lambda at, *_: (at, 0, 0, 0))],
            out_specs=[
                pl.BlockSpec((chunk, genes, BS), lambda at, *_: (at, 0, 0)),
                pl.BlockSpec((genes, BS), whole),
                pl.BlockSpec((genes, BS), whole),
            ],
            scratch_shapes=[
                pltpu.VMEM((n * size, genes, BS), pieces[0].dtype),
                pltpu.SemaphoreType.DMA((n,)),
            ],
        ),
        out_shape=[
            jax.ShapeDtypeStruct((blocks, genes, BS), out_type),
            jax.ShapeDtypeStruct((genes, BS), jnp.float32),
            jax.ShapeDtypeStruct((genes, BS), jnp.float32),
        ],
        compiler_params=pltpu.CompilerParams(vmem_limit_bytes=40 * 1024 * 1024),
        cost_estimate=pl.CostEstimate(
            flops=2 * blocks * slots * BS * BS * genes,
            bytes_accessed=2 * blocks * slots * BS * BS,
            transcendentals=0,
        ),
    )(places, counts, *pieces, affinity)


def to_all(value, axis, size):
    return lax.all_to_all(
        jnp.broadcast_to(value[None], (size,) + value.shape), axis, 0, 0, tiled=True
    )


def local(stored, neighbours, counts, affinity):
    core, my_x, my_y = lax.axis_index("c"), lax.axis_index("x"), lax.axis_index("y")
    blocks_dev, slots = neighbours.shape
    half = blocks_dev // 2
    part = lax.dynamic_slice_in_dim(affinity, core * half, half, 0)
    affinity = lax.all_gather(part, ("z", "c"), tiled=True)

    table = jnp.concatenate([neighbours, counts[:, None]], axis=1).reshape(-1)
    table = jnp.pad(table, (0, 128 - table.shape[0]))
    table = to_all(table, "z", GROUP)[:, : blocks_dev * (slots + 1)]
    table = table.reshape(GROUP * blocks_dev, slots + 1)
    neighbours, counts = table[:, :slots], table[:, slots]

    device, inner = neighbours // blocks_dev, neighbours % blocks_dev
    plane = device // (SIDE * SIDE)
    dx = (device // SIDE - my_x) % SIDE
    dy = (device - my_y) % SIDE
    half_group = GROUP // 2
    within = (plane % half_group) * blocks_dev + inner
    unit = half_group * blocks_dev
    places = jnp.where(
        plane < half_group,
        (dy * SIDE + dx) * unit + within,
        (SIDE * SIDE + dx * SIDE + dy) * unit + within,
    ).reshape(-1)

    genes_dev = stored.shape[0]
    cells_dev = blocks_dev * BS
    counted = stored.reshape(genes_dev, GROUP, SIDE * SIDE, cells_dev)
    counted = lax.all_to_all(counted, XY, 2, 0, tiled=True)
    genes = counted.shape[0]
    counted = counted.reshape(genes, GROUP * blocks_dev, BS).astype(jnp.float32)
    partial = lax.psum(jnp.sum(counted, axis=0), "c")
    library = jnp.sum(to_all(partial, "z", GROUP), axis=0) / (2 * GROUP * genes)
    current = (counted / library[None]).astype(jnp.bfloat16)
    current = jnp.transpose(current, (1, 0, 2))

    peaks = []
    for step in range(STEPS):
        current, peak, own_peak = diffuse(spread(current), places, counts, affinity, jnp.bfloat16)
        if step == 0:
            peaks.append(own_peak)
        peaks.append(peak)
    peaks = jnp.max(jnp.stack(peaks), axis=2).reshape(-1)
    peaks = jnp.max(to_all(peaks, XY, SIDE * SIDE), axis=0).reshape(STEPS + 1, genes)
    scale = jnp.ones((genes,), jnp.float32)
    for step in range(STEPS):
        scale = scale * (peaks[0] / (scale * peaks[1 + step] + epsilon))
    result = (current.astype(jnp.float32) * scale[None, :, None]).astype(jnp.bfloat16)
    result = jnp.transpose(result, (1, 0, 2)).reshape(genes, GROUP, cells_dev)
    result = lax.all_to_all(result, "z", 1, 0, tiled=True)
    return result.reshape(GROUP * genes, cells_dev).astype(jnp.float32)


def solution(mesh):
    grid = Mesh(mesh.devices.reshape(GROUP, SIDE, SIDE, 2), ("z", "x", "y", "c"))
    cells = ("z", "x", "y")
    return jax.shard_map(
        local,
        mesh=grid,
        in_specs=(P(cells, "c", None), P(cells, None), P(cells), P(cells, None, None, None)),
        out_specs=P("c", cells),
        check_vma=False,
    )
```

```python
import functools

import jax
import jax.numpy as jnp
from jax import lax
from jax.experimental import pallas as pl
from jax.experimental.pallas import tpu as pltpu
from jax.sharding import Mesh, PartitionSpec as P

REMOTE = 4
STEPS = 3
SIDE = 4
GROUP = 8
BS = 128
STREAMS = 2
UNROLL = 4
epsilon = 1e-06
XY = ("x", "y")


def shift(value, distance, stage):
    pairs = []
    for x in range(SIDE):
        for y in range(SIDE):
            for core in range(2):
                if core == stage:
                    source = ((x + distance) % SIDE) * SIDE + y
                else:
                    source = x * SIDE + (y + distance) % SIDE
                pairs.append((source * 2 + core, (x * SIDE + y) * 2 + core))
    return lax.ppermute(value, ("x", "y", "c"), pairs)


def pack_kernel(*refs):
    for i, source in enumerate(refs[:-1]):
        size = source.shape[0]
        refs[-1][pl.ds(i * size, size)] = source[...]


def pack(parts):
    size, genes, width = parts[0].shape
    return pl.pallas_call(
        pack_kernel,
        out_shape=jax.ShapeDtypeStruct((len(parts) * size, genes, width), parts[0].dtype),
        compiler_params=pltpu.CompilerParams(vmem_limit_bytes=16 * 1024 * 1024),
    )(*parts)


def spread(value, ring):
    value = pack([value] + [shift(value, d, 0) for d in (1, 2, 3)])
    if not ring:
        return [value] + [shift(value, d, 1) for d in (1, 2, 3)]
    half = value.shape[0] // 2
    after, before = shift(value, 1, 1), shift(value, 3, 1)
    low, high = shift(after[:half], 1, 1), shift(before[half:], 3, 1)
    return [value, after, low, high, before]


def step_kernel(pieces, raw, ends, place_ref, count_ref, table_ref, *refs):
    sources, refs = refs[:pieces], refs[pieces:]
    if raw:
        inverse_ref, refs = refs[0], refs[1:]
    aff_ref, out_refs, refs = refs[0], refs[1 : 1 + ends], refs[1 + ends :]
    peak_ref, own_peak_ref, held, kept, sems = refs
    blocks, slots = aff_ref.shape[:2]
    genes = held.shape[1]
    parts = 4
    size = blocks // parts

    def part(i):
        rows = pl.ds(i * size, size)
        return pltpu.make_async_copy(aff_ref.at[rows], kept.at[rows], sems.at[pieces + i])

    copies, start = [], 0
    for i, source in enumerate(sources):
        rows = source.shape[0]
        copies.append(pltpu.make_async_copy(source, held.at[pl.ds(start, rows)], sems.at[i]))
        start += rows
    part(0).start()
    for copy in copies:
        copy.start()
    for i in range(1, parts):
        part(i).start()
    for copy in copies:
        copy.wait()

    def fetch(item):
        tile = held[place_ref[item]]
        if raw:
            tile = tile.astype(jnp.float32) * inverse_ref[pl.ds(table_ref[item], 1), :]
            tile = tile.astype(jnp.bfloat16)
        return tile

    def one(row, peak, own_peak):
        count = count_ref[row]
        tiles = []
        for s in range(slots):
            tile = fetch(row * slots + s)
            if s == 0:
                own = tile.astype(jnp.float32)
            tile = jnp.concatenate([tile, jnp.ones((16, BS), tile.dtype)], axis=0)
            if s > REMOTE:
                tile = jnp.where(s < count, tile, jnp.zeros_like(tile))
            tiles.append(tile)
        left = jnp.concatenate(tiles, axis=1)
        right = kept[row].reshape(slots * BS, BS)
        total = jnp.dot(left, right, preferred_element_type=jnp.float32)
        mixed = 0.5 * own + total[:genes] * (0.5 / total[genes : genes + 1])
        for out_ref in out_refs:
            share = out_ref.shape[1]
            out_ref[row] = mixed[:share].astype(out_ref.dtype)
            mixed = jnp.concatenate([mixed[share:], mixed[:share]]) if ends > 1 else mixed
        return jnp.maximum(peak, mixed), jnp.maximum(own_peak, own)

    def several(i, carry):
        for j in range(UNROLL):
            carry = one(i * UNROLL + j, *carry)
        return carry

    carry = (jnp.zeros((genes, BS), jnp.float32),) * 2
    for i in range(parts):
        part(i).wait()
        each = size // UNROLL
        carry = lax.fori_loop(i * each, (i + 1) * each, several, carry)
    peak_ref[...], own_peak_ref[...] = carry


def diffuse(pieces, places, counts, tables, inverse, affinity, ends):
    blocks = affinity.shape[0]
    genes = pieces[0].shape[1]
    total = sum(piece.shape[0] for piece in pieces)
    n = len(pieces)
    raw = inverse is not None
    smem = pl.BlockSpec(memory_space=pltpu.SMEM)
    vmem = pl.BlockSpec(memory_space=pltpu.VMEM)
    return pl.pallas_call(
        functools.partial(step_kernel, n, raw, ends),
        in_specs=[smem] * 3
        + [pl.BlockSpec(memory_space=pl.ANY)] * n
        + [vmem] * raw
        + [pl.BlockSpec(memory_space=pl.ANY)],
        out_specs=[vmem] * (ends + 2),
        scratch_shapes=[
            pltpu.VMEM((total, genes, BS), pieces[0].dtype),
            pltpu.VMEM(affinity.shape, affinity.dtype),
            pltpu.SemaphoreType.DMA((n + 4,)),
        ],
        out_shape=[jax.ShapeDtypeStruct((blocks, genes // ends, BS), jnp.bfloat16)] * ends
        + [jax.ShapeDtypeStruct((genes, BS), jnp.float32)] * 2,
        compiler_params=pltpu.CompilerParams(vmem_limit_bytes=32 * 1024 * 1024),
        cost_estimate=pl.CostEstimate(
            flops=2 * affinity.size * genes,
            bytes_accessed=2 * affinity.size,
            transcendentals=0,
        ),
    )(places, counts, tables, *pieces, *([inverse] if raw else []), affinity)


def to_all(value, axis, size):
    return lax.all_to_all(
        jnp.broadcast_to(value[None], (size,) + value.shape), axis, 0, 0, tiled=True
    )


def local(stored, neighbours, counts, affinity):
    core, my_x, my_y = lax.axis_index("c"), lax.axis_index("x"), lax.axis_index("y")
    blocks_dev, slots = neighbours.shape
    part = lax.dynamic_slice_in_dim(affinity, core * (blocks_dev // 2), blocks_dev // 2, 0)
    affinity = lax.all_gather(part, ("z", "c"), tiled=True)

    genes_dev = stored.shape[0]
    cells_dev = blocks_dev * BS
    blocks = GROUP * blocks_dev
    counted = stored.reshape(genes_dev, GROUP, SIDE * SIDE, cells_dev)
    counted = lax.all_to_all(counted, XY, 2, 0, tiled=True)
    genes = counted.shape[0]
    counted = jnp.transpose(counted.reshape(genes, blocks, BS), (1, 0, 2))

    table = jnp.concatenate([neighbours, counts[:, None]], axis=1).reshape(1, -1)
    used = table.shape[1]
    table = jnp.pad(table.astype(jnp.float32), ((0, 7), (0, BS - used)))
    sums = lax.psum(jnp.sum(counted.astype(jnp.float32), axis=1), "c")
    sums = to_all(jnp.concatenate([sums, table]), "z", GROUP)
    inverse = (2 * GROUP * genes) / jnp.sum(sums[:, :blocks], axis=0)
    inverse = to_all(inverse, XY, SIDE * SIDE).reshape(-1, BS)
    table = sums[:, blocks, :used].astype(jnp.int32).reshape(blocks, slots + 1)
    neighbours, counts = table[:, :slots], table[:, slots]

    device, inner = neighbours // blocks_dev, neighbours % blocks_dev
    within = device // (SIDE * SIDE) * blocks_dev + inner
    dx = (device // SIDE - my_x) % SIDE
    dy = (device - my_y) % SIDE
    first, second = jnp.where(core == 0, dx, dy), jnp.where(core == 0, dy, dx)
    places = ((second * SIDE + first) * blocks + within).reshape(-1)
    tables = ((device % (SIDE * SIDE)) * blocks + within).reshape(-1)

    *streams, peak, own_peak = diffuse(
        spread(counted, False), places, counts, tables, inverse, affinity, STREAMS
    )
    peaks = [own_peak, peak]
    for step in range(1, STEPS):
        pieces = [spread(stream, True) for stream in streams]
        ends = [diffuse(piece, places, counts, tables, None, affinity, 1) for piece in pieces]
        streams = [end[0] for end in ends]
        peaks.append(jnp.concatenate([end[1] for end in ends]))
    current = jnp.concatenate(streams, axis=1)
    peaks = jnp.max(jnp.stack(peaks), axis=2).reshape(-1)
    peaks = jnp.max(to_all(peaks, XY, SIDE * SIDE), axis=0).reshape(STEPS + 1, genes)
    scale = jnp.ones((genes,), jnp.float32)
    for step in range(STEPS):
        scale = scale * (peaks[0] / (scale * peaks[1 + step] + epsilon))
    result = (current.astype(jnp.float32) * scale[None, :, None]).astype(jnp.bfloat16)
    result = lax.all_to_all(result, "z", 0, 0, tiled=True)
    result = result.reshape(GROUP, blocks_dev, genes, BS).astype(jnp.float32)
    return jnp.transpose(result, (0, 2, 1, 3)).reshape(GROUP * genes, cells_dev)


def solution(mesh):
    grid = Mesh(mesh.devices.reshape(GROUP, SIDE, SIDE, 2), ("z", "x", "y", "c"))
    cells = ("z", "x", "y")
    return jax.shard_map(
        local,
        mesh=grid,
        in_specs=(P(cells, "c", None), P(cells, None), P(cells), P(cells, None, None, None)),
        out_specs=P("c", cells),
        check_vma=False,
    )
```

```python
import functools

import jax
import jax.numpy as jnp
from jax import lax
from jax.experimental import pallas as pl
from jax.experimental.pallas import tpu as pltpu
from jax.sharding import Mesh, PartitionSpec as P

REMOTE = 4
STEPS = 3
SIDE = 4
GROUP = 8
BS = 128
STREAMS = 2
UNROLL = 4
epsilon = 1e-06
XY = ("x", "y")


def shift(value, distance, stage):
    pairs = []
    for x in range(SIDE):
        for y in range(SIDE):
            for core in range(2):
                if core == stage:
                    source = ((x + distance) % SIDE) * SIDE + y
                else:
                    source = x * SIDE + (y + distance) % SIDE
                pairs.append((source * 2 + core, (x * SIDE + y) * 2 + core))
    return lax.ppermute(value, ("x", "y", "c"), pairs)


def pack_kernel(parts, *refs):
    for i, source in enumerate(refs[:parts]):
        size = source.shape[0]
        for j, out_ref in enumerate(refs[parts:]):
            share = out_ref.shape[1]
            out_ref[pl.ds(i * size, size)] = source[:, j * share : (j + 1) * share]


def pack(parts, ends):
    size, genes, width = parts[0].shape
    shape = jax.ShapeDtypeStruct((len(parts) * size, genes // ends, width), parts[0].dtype)
    return pl.pallas_call(
        functools.partial(pack_kernel, len(parts)),
        out_shape=[shape] * ends,
        compiler_params=pltpu.CompilerParams(vmem_limit_bytes=16 * 1024 * 1024),
    )(*parts)


def line(value, ends):
    return pack([value] + [shift(value, d, 0) for d in (1, 2, 3)], ends)


def plane(value, ring):
    if not ring:
        return [value] + [shift(value, d, 1) for d in (1, 2, 3)]
    half = value.shape[0] // 2
    after, before = shift(value, 1, 1), shift(value, 3, 1)
    low, high = shift(after[:half], 1, 1), shift(before[half:], 3, 1)
    return [value, after, low, high, before]


def step_kernel(pieces, raw, ends, place_ref, count_ref, table_ref, *refs):
    sources, refs = refs[:pieces], refs[pieces:]
    if raw:
        inverse_ref, refs = refs[0], refs[1:]
    aff_ref, out_refs, refs = refs[0], refs[1 : 1 + ends], refs[1 + ends :]
    peak_ref, refs = refs[0], refs[1:]
    if raw:
        own_peak_ref, refs = refs[0], refs[1:]
    held, sems = refs
    blocks, slots = aff_ref.shape[:2]
    genes = held.shape[1]
    copies, start = [], 0
    for i, source in enumerate(sources):
        rows = source.shape[0]
        copies.append(pltpu.make_async_copy(source, held.at[pl.ds(start, rows)], sems.at[i]))
        start += rows
    for copy in copies:
        copy.start()
    for copy in copies:
        copy.wait()

    def fetch(item):
        tile = held[place_ref[item]]
        if raw:
            tile = tile.astype(jnp.float32) * inverse_ref[pl.ds(table_ref[item], 1), :]
            tile = tile.astype(jnp.bfloat16)
        return tile

    def one(row, peaks):
        count = count_ref[row]
        tiles = []
        for s in range(slots):
            tile = fetch(row * slots + s)
            if s == 0:
                own = tile.astype(jnp.float32)
            tile = jnp.concatenate([tile, jnp.ones((16, BS), tile.dtype)], axis=0)
            if s > REMOTE:
                tile = jnp.where(s < count, tile, jnp.zeros_like(tile))
            tiles.append(tile)
        left = jnp.concatenate(tiles, axis=1)
        right = aff_ref[row].reshape(slots * BS, BS)
        total = jnp.dot(left, right, preferred_element_type=jnp.float32)
        mixed = 0.5 * own + total[:genes] * (0.5 / total[genes : genes + 1])
        for out_ref in out_refs:
            share = out_ref.shape[1]
            out_ref[row] = mixed[:share].astype(out_ref.dtype)
            mixed = jnp.concatenate([mixed[share:], mixed[:share]]) if ends > 1 else mixed
        found = (mixed, own) if raw else (mixed,)
        return tuple(jnp.maximum(a, b) for a, b in zip(peaks, found))

    def several(i, carry):
        for j in range(UNROLL):
            carry = one(i * UNROLL + j, carry)
        return carry

    carry = (jnp.zeros((genes, BS), jnp.float32),) * (1 + raw)
    carry = lax.fori_loop(0, blocks // UNROLL, several, carry)
    peak_ref[...] = carry[0]
    if raw:
        own_peak_ref[...] = carry[1]


def diffuse(pieces, places, counts, tables, inverse, affinity, ends):
    blocks = affinity.shape[0]
    genes = pieces[0].shape[1]
    total = sum(piece.shape[0] for piece in pieces)
    n = len(pieces)
    raw = inverse is not None
    smem = pl.BlockSpec(memory_space=pltpu.SMEM)
    vmem = pl.BlockSpec(memory_space=pltpu.VMEM)
    return pl.pallas_call(
        functools.partial(step_kernel, n, raw, ends),
        in_specs=[smem] * 3
        + [pl.BlockSpec(memory_space=pl.ANY)] * n
        + [vmem] * raw
        + [vmem],
        out_specs=[vmem] * (ends + 1 + raw),
        scratch_shapes=[
            pltpu.VMEM((total, genes, BS), pieces[0].dtype),
            pltpu.SemaphoreType.DMA((n,)),
        ],
        out_shape=[jax.ShapeDtypeStruct((blocks, genes // ends, BS), jnp.bfloat16)] * ends
        + [jax.ShapeDtypeStruct((genes, BS), jnp.float32)] * (1 + raw),
        compiler_params=pltpu.CompilerParams(vmem_limit_bytes=32 * 1024 * 1024),
        cost_estimate=pl.CostEstimate(
            flops=2 * affinity.size * genes,
            bytes_accessed=2 * affinity.size,
            transcendentals=0,
        ),
    )(places, counts, tables, *pieces, *([inverse] if raw else []), affinity)


def to_all(value, axis, size):
    return lax.all_to_all(
        jnp.broadcast_to(value[None], (size,) + value.shape), axis, 0, 0, tiled=True
    )


def local(stored, neighbours, counts, affinity):
    core, my_x, my_y = lax.axis_index("c"), lax.axis_index("x"), lax.axis_index("y")
    blocks_dev, slots = neighbours.shape
    part = lax.dynamic_slice_in_dim(affinity, core * (blocks_dev // 2), blocks_dev // 2, 0)
    affinity = lax.all_gather(part, ("z", "c"), tiled=True)

    genes_dev = stored.shape[0]
    cells_dev = blocks_dev * BS
    blocks = GROUP * blocks_dev
    counted = stored.reshape(genes_dev, GROUP, SIDE * SIDE, cells_dev)
    counted = lax.all_to_all(counted, XY, 2, 0, tiled=True)
    genes = counted.shape[0]
    counted = jnp.transpose(counted.reshape(genes, blocks, BS), (1, 0, 2))

    table = jnp.concatenate([neighbours, counts[:, None]], axis=1).reshape(1, -1)
    used = table.shape[1]
    table = jnp.pad(table.astype(jnp.float32), ((0, 7), (0, BS - used)))
    sums = lax.psum(jnp.sum(counted.astype(jnp.float32), axis=1), "c")
    sums = to_all(jnp.concatenate([sums, table]), "z", GROUP)
    inverse = (2 * GROUP * genes) / jnp.sum(sums[:, :blocks], axis=0)
    inverse = to_all(inverse, XY, SIDE * SIDE).reshape(-1, BS)
    table = sums[:, blocks, :used].astype(jnp.int32).reshape(blocks, slots + 1)
    neighbours, counts = table[:, :slots], table[:, slots]

    device, inner = neighbours // blocks_dev, neighbours % blocks_dev
    within = device // (SIDE * SIDE) * blocks_dev + inner
    dx = (device // SIDE - my_x) % SIDE
    dy = (device - my_y) % SIDE
    first, second = jnp.where(core == 0, dx, dy), jnp.where(core == 0, dy, dx)
    places = ((second * SIDE + first) * blocks + within).reshape(-1)
    tables = ((device % (SIDE * SIDE)) * blocks + within).reshape(-1)

    current, peak, own_peak = diffuse(
        plane(*line(counted, 1), False), places, counts, tables, inverse, affinity, 1
    )
    peaks = [own_peak, peak]
    lines = line(current, STREAMS)
    for step in range(1, STEPS):
        if step > 1:
            lines = [line(stream, 1)[0] for stream in streams]
        ends = [
            diffuse(plane(part, True), places, counts, tables, None, affinity, 1) for part in lines
        ]
        streams = [end[0] for end in ends]
        peaks.append(jnp.concatenate([end[1] for end in ends]))
    current = jnp.concatenate(streams, axis=1)
    peaks = jnp.max(jnp.stack(peaks), axis=2).reshape(-1)
    peaks = jnp.max(to_all(peaks, XY, SIDE * SIDE), axis=0).reshape(STEPS + 1, genes)
    scale = jnp.ones((genes,), jnp.float32)
    for step in range(STEPS):
        scale = scale * (peaks[0] / (scale * peaks[1 + step] + epsilon))
    result = (current.astype(jnp.float32) * scale[None, :, None]).astype(jnp.bfloat16)
    result = lax.all_to_all(result, "z", 0, 0, tiled=True)
    result = result.reshape(GROUP, blocks_dev, genes, BS).astype(jnp.float32)
    return jnp.transpose(result, (0, 2, 1, 3)).reshape(GROUP * genes, cells_dev)


def solution(mesh):
    grid = Mesh(mesh.devices.reshape(GROUP, SIDE, SIDE, 2), ("z", "x", "y", "c"))
    cells = ("z", "x", "y")
    return jax.shard_map(
        local,
        mesh=grid,
        in_specs=(P(cells, "c", None), P(cells, None), P(cells), P(cells, None, None, None)),
        out_specs=P("c", cells),
        check_vma=False,
    )
```

```python
import functools

import jax
import jax.numpy as jnp
from jax import lax
from jax.experimental import pallas as pl
from jax.experimental.pallas import tpu as pltpu
from jax.sharding import Mesh, PartitionSpec as P

REMOTE = 4
STEPS = 3
SIDE = 4
GROUP = 8
BS = 128
STREAMS = 2
UNROLL = 16
epsilon = 1e-06
XY = ("x", "y")


def shift(value, distance, stage):
    pairs = []
    for x in range(SIDE):
        for y in range(SIDE):
            for core in range(2):
                if core == stage:
                    source = ((x + distance) % SIDE) * SIDE + y
                else:
                    source = x * SIDE + (y + distance) % SIDE
                pairs.append((source * 2 + core, (x * SIDE + y) * 2 + core))
    return lax.ppermute(value, ("x", "y", "c"), pairs)


def pack_kernel(parts, *refs):
    for i, source in enumerate(refs[:parts]):
        size = source.shape[0]
        for j, out_ref in enumerate(refs[parts:]):
            share = out_ref.shape[1]
            out_ref[pl.ds(i * size, size)] = source[:, j * share : (j + 1) * share]


def pack(parts, ends):
    size, genes, width = parts[0].shape
    shape = jax.ShapeDtypeStruct((len(parts) * size, genes // ends, width), parts[0].dtype)
    return pl.pallas_call(
        functools.partial(pack_kernel, len(parts)),
        out_shape=[shape] * ends,
        compiler_params=pltpu.CompilerParams(vmem_limit_bytes=16 * 1024 * 1024),
    )(*parts)


def line(value, ends):
    return pack([value] + [shift(value, d, 0) for d in (1, 2, 3)], ends)


def plane(value, ring):
    if not ring:
        return [value] + [shift(value, d, 1) for d in (1, 2, 3)]
    half = value.shape[0] // 2
    after, before = shift(value, 1, 1), shift(value, 3, 1)
    low, high = shift(after[:half], 1, 1), shift(before[half:], 3, 1)
    return [value, after, low, high, before]


def step_kernel(pieces, raw, ends, place_ref, count_ref, table_ref, *refs):
    sources, refs = refs[:pieces], refs[pieces:]
    if raw:
        inverse_ref, refs = refs[0], refs[1:]
    else:
        share_ref, refs = refs[0], refs[1:]
    aff_ref, out_refs, refs = refs[0], refs[1 : 1 + ends], refs[1 + ends :]
    peak_ref, refs = refs[0], refs[1:]
    if raw:
        own_peak_ref, refs = refs[0], refs[1:]
        share_ref, refs = refs[0], refs[1:]
    held, sems = refs
    blocks, slots = aff_ref.shape[:2]
    genes = held.shape[1]
    copies, start = [], 0
    for i, source in enumerate(sources):
        rows = source.shape[0]
        copies.append(pltpu.make_async_copy(source, held.at[pl.ds(start, rows)], sems.at[i]))
        start += rows
    for copy in copies:
        copy.start()
    for copy in copies:
        copy.wait()

    def fetch(item):
        tile = held[place_ref[item]]
        if raw:
            tile = tile.astype(jnp.float32) * inverse_ref[pl.ds(table_ref[item], 1), :]
            tile = tile.astype(jnp.bfloat16)
        return tile

    def one(row, peaks):
        count = count_ref[row]
        tiles = []
        for s in range(slots):
            tile = fetch(row * slots + s)
            if s == 0:
                own = tile.astype(jnp.float32)
            if raw:
                tile = jnp.concatenate([tile, jnp.ones((16, BS), tile.dtype)], axis=0)
            if s > REMOTE:
                tile = jnp.where(s < count, tile, jnp.zeros_like(tile))
            tiles.append(tile)
        left = jnp.concatenate(tiles, axis=1)
        right = aff_ref[row].reshape(slots * BS, BS)
        total = jnp.dot(left, right, preferred_element_type=jnp.float32)
        if raw:
            share_ref[pl.ds(row, 1)] = 0.5 / total[genes : genes + 1]
        mixed = 0.5 * own + total[:genes] * share_ref[pl.ds(row, 1)]
        for out_ref in out_refs:
            share = out_ref.shape[1]
            out_ref[row] = mixed[:share].astype(out_ref.dtype)
            mixed = jnp.concatenate([mixed[share:], mixed[:share]]) if ends > 1 else mixed
        found = (mixed, own) if raw else (mixed,)
        return tuple(jnp.maximum(a, b) for a, b in zip(peaks, found))

    def several(i, carry):
        for j in range(UNROLL):
            carry = one(i * UNROLL + j, carry)
        return carry

    carry = (jnp.zeros((genes, BS), jnp.float32),) * (1 + raw)
    carry = lax.fori_loop(0, blocks // UNROLL, several, carry)
    peak_ref[...] = carry[0]
    if raw:
        own_peak_ref[...] = carry[1]


def diffuse(pieces, places, counts, tables, inverse, share, affinity, ends):
    blocks = affinity.shape[0]
    genes = pieces[0].shape[1]
    total = sum(piece.shape[0] for piece in pieces)
    n = len(pieces)
    raw = inverse is not None
    smem = pl.BlockSpec(memory_space=pltpu.SMEM)
    vmem = pl.BlockSpec(memory_space=pltpu.VMEM)
    return pl.pallas_call(
        functools.partial(step_kernel, n, raw, ends),
        in_specs=[smem] * 3
        + [pl.BlockSpec(memory_space=pl.ANY)] * n
        + [vmem]
        + [vmem],
        out_specs=[vmem] * (ends + 1 + 2 * raw),
        scratch_shapes=[
            pltpu.VMEM((total, genes, BS), pieces[0].dtype),
            pltpu.SemaphoreType.DMA((n,)),
        ],
        out_shape=[jax.ShapeDtypeStruct((blocks, genes // ends, BS), jnp.bfloat16)] * ends
        + [jax.ShapeDtypeStruct((genes, BS), jnp.float32)] * (1 + raw)
        + [jax.ShapeDtypeStruct((blocks, BS), jnp.float32)] * raw,
        compiler_params=pltpu.CompilerParams(vmem_limit_bytes=32 * 1024 * 1024),
        cost_estimate=pl.CostEstimate(
            flops=2 * affinity.size * genes,
            bytes_accessed=2 * affinity.size,
            transcendentals=0,
        ),
    )(places, counts, tables, *pieces, inverse if raw else share, affinity)


def to_all(value, axis, size):
    return lax.all_to_all(
        jnp.broadcast_to(value[None], (size,) + value.shape), axis, 0, 0, tiled=True
    )


def local(stored, neighbours, counts, affinity):
    core, my_x, my_y = lax.axis_index("c"), lax.axis_index("x"), lax.axis_index("y")
    blocks_dev, slots = neighbours.shape
    part = lax.dynamic_slice_in_dim(affinity, core * (blocks_dev // 2), blocks_dev // 2, 0)
    affinity = lax.all_gather(part, ("z", "c"), tiled=True)

    genes_dev = stored.shape[0]
    cells_dev = blocks_dev * BS
    blocks = GROUP * blocks_dev
    counted = stored.reshape(genes_dev, GROUP, SIDE * SIDE, cells_dev)
    counted = lax.all_to_all(counted, XY, 2, 0, tiled=True)
    genes = counted.shape[0]
    counted = jnp.transpose(counted.reshape(genes, blocks, BS), (1, 0, 2))

    table = jnp.concatenate([neighbours, counts[:, None]], axis=1).reshape(1, -1)
    used = table.shape[1]
    table = jnp.pad(table.astype(jnp.float32), ((0, 7), (0, BS - used)))
    sums = lax.psum(jnp.sum(counted.astype(jnp.float32), axis=1), "c")
    sums = to_all(jnp.concatenate([sums, table]), "z", GROUP)
    inverse = (2 * GROUP * genes) / jnp.sum(sums[:, :blocks], axis=0)
    inverse = to_all(inverse, XY, SIDE * SIDE).reshape(-1, BS)
    table = sums[:, blocks, :used].astype(jnp.int32).reshape(blocks, slots + 1)
    neighbours, counts = table[:, :slots], table[:, slots]

    device, inner = neighbours // blocks_dev, neighbours % blocks_dev
    within = device // (SIDE * SIDE) * blocks_dev + inner
    dx = (device // SIDE - my_x) % SIDE
    dy = (device - my_y) % SIDE
    first, second = jnp.where(core == 0, dx, dy), jnp.where(core == 0, dy, dx)
    places = ((second * SIDE + first) * blocks + within).reshape(-1)
    tables = ((device % (SIDE * SIDE)) * blocks + within).reshape(-1)

    current, peak, own_peak, share = diffuse(
        plane(*line(counted, 1), False), places, counts, tables, inverse, None, affinity, 1
    )
    peaks = [own_peak, peak]
    lines = line(current, STREAMS)
    for step in range(1, STEPS):
        if step > 1:
            lines = [line(stream, 1)[0] for stream in streams]
        ends = [
            diffuse(plane(part, True), places, counts, tables, None, share, affinity, 1) for part in lines
        ]
        streams = [end[0] for end in ends]
        peaks.append(jnp.concatenate([end[1] for end in ends]))
    current = jnp.concatenate(streams, axis=1)
    peaks = jnp.max(jnp.stack(peaks), axis=2).reshape(-1)
    peaks = jnp.max(to_all(peaks, XY, SIDE * SIDE), axis=0).reshape(STEPS + 1, genes)
    scale = jnp.ones((genes,), jnp.float32)
    for step in range(STEPS):
        scale = scale * (peaks[0] / (scale * peaks[1 + step] + epsilon))
    result = (current.astype(jnp.float32) * scale[None, :, None]).astype(jnp.bfloat16)
    result = lax.all_to_all(result, "z", 0, 0, tiled=True)
    result = result.reshape(GROUP, blocks_dev, genes, BS).astype(jnp.float32)
    return jnp.transpose(result, (0, 2, 1, 3)).reshape(GROUP * genes, cells_dev)


def solution(mesh):
    grid = Mesh(mesh.devices.reshape(GROUP, SIDE, SIDE, 2), ("z", "x", "y", "c"))
    cells = ("z", "x", "y")
    return jax.shard_map(
        local,
        mesh=grid,
        in_specs=(P(cells, "c", None), P(cells, None), P(cells), P(cells, None, None, None)),
        out_specs=P("c", cells),
        check_vma=False,
    )
```

```python
import functools

import jax
import jax.numpy as jnp
from jax import lax
from jax.experimental import pallas as pl
from jax.experimental.pallas import tpu as pltpu
from jax.sharding import Mesh, PartitionSpec as P

REMOTE = 4
STEPS = 3
SIDE = 4
GROUP = 8
BS = 128
STREAMS = 2
UNROLL = 16
epsilon = 1e-06
XY = ("x", "y")


def shift(value, distance, stage):
    pairs = []
    for x in range(SIDE):
        for y in range(SIDE):
            for core in range(2):
                if core == stage:
                    source = ((x + distance) % SIDE) * SIDE + y
                else:
                    source = x * SIDE + (y + distance) % SIDE
                pairs.append((source * 2 + core, (x * SIDE + y) * 2 + core))
    return lax.ppermute(value, ("x", "y", "c"), pairs)


def pack_kernel(parts, *refs):
    for i, source in enumerate(refs[:parts]):
        size = source.shape[0]
        for j, out_ref in enumerate(refs[parts:]):
            share = out_ref.shape[1]
            out_ref[pl.ds(i * size, size)] = source[:, j * share : (j + 1) * share]


def pack(parts, ends):
    size, genes, width = parts[0].shape
    shape = jax.ShapeDtypeStruct((len(parts) * size, genes // ends, width), parts[0].dtype)
    return pl.pallas_call(
        functools.partial(pack_kernel, len(parts)),
        out_shape=[shape] * ends,
        compiler_params=pltpu.CompilerParams(vmem_limit_bytes=16 * 1024 * 1024),
    )(*parts)


def line(value, ends):
    return pack([value] + [shift(value, d, 0) for d in (1, 2, 3)], ends)


def plane(value, ring):
    if not ring:
        return [value] + [shift(value, d, 1) for d in (1, 2, 3)]
    half = value.shape[0] // 2
    after, before = shift(value, 1, 1), shift(value, 3, 1)
    low, high = shift(after[:half], 1, 1), shift(before[half:], 3, 1)
    return [value, after, low, high, before]


def step_kernel(pieces, raw, ends, place_ref, count_ref, table_ref, *refs):
    sources, refs = refs[:pieces], refs[pieces:]
    if raw:
        inverse_ref, refs = refs[0], refs[1:]
    else:
        share_ref, refs = refs[0], refs[1:]
    aff_ref, out_refs, refs = refs[0], refs[1 : 1 + ends], refs[1 + ends :]
    peak_ref, refs = refs[0], refs[1:]
    if raw:
        own_peak_ref, refs = refs[0], refs[1:]
        share_ref, refs = refs[0], refs[1:]
    held, sems = refs
    blocks, slots = aff_ref.shape[:2]
    genes = held.shape[1]
    copies, start = [], 0
    for i, source in enumerate(sources):
        rows = source.shape[0]
        copies.append(pltpu.make_async_copy(source, held.at[pl.ds(start, rows)], sems.at[i]))
        start += rows
    for copy in copies:
        copy.start()
    for copy in copies:
        copy.wait()

    def fetch(item):
        tile = held[place_ref[item]]
        if raw:
            tile = tile.astype(jnp.float32) * inverse_ref[pl.ds(table_ref[item], 1), :]
            tile = tile.astype(jnp.bfloat16)
        return tile

    def one(row, peaks):
        count = count_ref[row]
        tiles = []
        for s in range(slots):
            tile = fetch(row * slots + s)
            if s == 0:
                own = tile.astype(jnp.float32)
            if raw:
                tile = jnp.concatenate([tile, jnp.ones((16, BS), tile.dtype)], axis=0)
            if s > REMOTE:
                tile = jnp.where(s < count, tile, jnp.zeros_like(tile))
            tiles.append(tile)
        left = jnp.concatenate(tiles, axis=1)
        right = aff_ref[row].reshape(slots * BS, BS)
        total = jnp.dot(left, right, preferred_element_type=jnp.float32)
        if raw:
            share_ref[pl.ds(row, 1)] = 0.5 / total[genes : genes + 1]
        mixed = 0.5 * own + total[:genes] * share_ref[pl.ds(row, 1)]
        for out_ref in out_refs:
            share = out_ref.shape[1]
            out_ref[row] = mixed[:share].astype(out_ref.dtype)
            mixed = jnp.concatenate([mixed[share:], mixed[:share]]) if ends > 1 else mixed
        found = (mixed, own) if raw else (mixed,)
        return tuple(jnp.maximum(a, b) for a, b in zip(peaks, found))

    def several(i, carry):
        for j in range(UNROLL):
            carry = one(i * UNROLL + j, carry)
        return carry

    carry = (jnp.zeros((genes, BS), jnp.float32),) * (1 + raw)
    carry = lax.fori_loop(0, blocks // UNROLL, several, carry)
    peak_ref[...] = carry[0]
    if raw:
        own_peak_ref[...] = carry[1]


def diffuse(pieces, places, counts, tables, inverse, share, affinity, ends):
    blocks = affinity.shape[0]
    genes = pieces[0].shape[1]
    total = sum(piece.shape[0] for piece in pieces)
    n = len(pieces)
    raw = inverse is not None
    smem = pl.BlockSpec(memory_space=pltpu.SMEM)
    vmem = pl.BlockSpec(memory_space=pltpu.VMEM)
    return pl.pallas_call(
        functools.partial(step_kernel, n, raw, ends),
        in_specs=[smem] * 3
        + [pl.BlockSpec(memory_space=pl.ANY)] * n
        + [vmem]
        + [vmem],
        out_specs=[vmem] * (ends + 1 + 2 * raw),
        scratch_shapes=[
            pltpu.VMEM((total, genes, BS), pieces[0].dtype),
            pltpu.SemaphoreType.DMA((n,)),
        ],
        out_shape=[jax.ShapeDtypeStruct((blocks, genes // ends, BS), jnp.bfloat16)] * ends
        + [jax.ShapeDtypeStruct((genes, BS), jnp.float32)] * (1 + raw)
        + [jax.ShapeDtypeStruct((blocks, BS), jnp.float32)] * raw,
        compiler_params=pltpu.CompilerParams(vmem_limit_bytes=32 * 1024 * 1024),
        cost_estimate=pl.CostEstimate(
            flops=2 * affinity.size * genes,
            bytes_accessed=2 * affinity.size,
            transcendentals=0,
        ),
    )(places, counts, tables, *pieces, inverse if raw else share, affinity)


def to_all(value, axis, size):
    return lax.all_to_all(
        jnp.broadcast_to(value[None], (size,) + value.shape), axis, 0, 0, tiled=True
    )


def local(stored, neighbours, counts, affinity):
    core, my_x, my_y = lax.axis_index("c"), lax.axis_index("x"), lax.axis_index("y")
    blocks_dev, slots = neighbours.shape
    part = lax.dynamic_slice_in_dim(affinity, core * (blocks_dev // 2), blocks_dev // 2, 0)
    affinity = lax.all_gather(part, ("z", "c"), tiled=True)

    genes_dev = stored.shape[0]
    cells_dev = blocks_dev * BS
    blocks = GROUP * blocks_dev
    counted = stored.reshape(genes_dev, GROUP, SIDE * SIDE, cells_dev)
    counted = lax.all_to_all(counted, XY, 2, 0, tiled=True)
    genes = counted.shape[0]
    counted = jnp.transpose(counted.reshape(genes, blocks, BS), (1, 0, 2))

    table = jnp.concatenate([neighbours, counts[:, None]], axis=1).reshape(1, -1)
    used = table.shape[1]
    table = jnp.pad(table.astype(jnp.float32), ((0, 7), (0, BS - used)))
    sums = jnp.sum(counted.astype(jnp.float32), axis=1)
    sums = sums + lax.ppermute(sums, "c", [(0, 1), (1, 0)])
    sums = to_all(jnp.concatenate([sums, table]), "z", GROUP)
    inverse = (2 * GROUP * genes) / jnp.sum(sums[:, :blocks], axis=0)
    inverse = to_all(inverse, XY, SIDE * SIDE).reshape(-1, BS)
    table = sums[:, blocks, :used].astype(jnp.int32).reshape(blocks, slots + 1)
    neighbours, counts = table[:, :slots], table[:, slots]

    device, inner = neighbours // blocks_dev, neighbours % blocks_dev
    within = device // (SIDE * SIDE) * blocks_dev + inner
    dx = (device // SIDE - my_x) % SIDE
    dy = (device - my_y) % SIDE
    first, second = jnp.where(core == 0, dx, dy), jnp.where(core == 0, dy, dx)
    places = ((second * SIDE + first) * blocks + within).reshape(-1)
    tables = ((device % (SIDE * SIDE)) * blocks + within).reshape(-1)

    current, peak, own_peak, share = diffuse(
        plane(*line(counted, 1), False), places, counts, tables, inverse, None, affinity, 1
    )
    peaks = [own_peak, peak]
    lines = line(current, STREAMS)
    for step in range(1, STEPS):
        if step > 1:
            lines = [line(stream, 1)[0] for stream in streams]
        ends = [
            diffuse(plane(part, True), places, counts, tables, None, share, affinity, 1) for part in lines
        ]
        streams = [end[0] for end in ends]
        peaks.append(jnp.concatenate([end[1] for end in ends]))
    current = jnp.concatenate(streams, axis=1)
    peaks = jnp.max(jnp.stack(peaks), axis=2).reshape(-1)
    peaks = jnp.max(to_all(peaks, XY, SIDE * SIDE), axis=0).reshape(STEPS + 1, genes)
    scale = jnp.ones((genes,), jnp.float32)
    for step in range(STEPS):
        scale = scale * (peaks[0] / (scale * peaks[1 + step] + epsilon))
    result = (current.astype(jnp.float32) * scale[None, :, None]).astype(jnp.bfloat16)
    result = lax.all_to_all(result, "z", 0, 0, tiled=True)
    result = result.reshape(GROUP, blocks_dev, genes, BS).astype(jnp.float32)
    return jnp.transpose(result, (0, 2, 1, 3)).reshape(GROUP * genes, cells_dev)


def solution(mesh):
    grid = Mesh(mesh.devices.reshape(GROUP, SIDE, SIDE, 2), ("z", "x", "y", "c"))
    cells = ("z", "x", "y")
    return jax.shard_map(
        local,
        mesh=grid,
        in_specs=(P(cells, "c", None), P(cells, None), P(cells), P(cells, None, None, None)),
        out_specs=P("c", cells),
        check_vma=False,
    )
```

```python
import functools

import jax
import jax.numpy as jnp
from jax import lax
from jax.experimental import pallas as pl
from jax.experimental.pallas import tpu as pltpu
from jax.sharding import Mesh, PartitionSpec as P

REMOTE = 4
STEPS = 3
SIDE = 4
GROUP = 8
BS = 128
STREAMS = 2
UNROLL = 32
epsilon = 1e-06
XY = ("x", "y")


def shift(value, distance, stage):
    pairs = []
    for x in range(SIDE):
        for y in range(SIDE):
            for core in range(2):
                if core == stage:
                    source = ((x + distance) % SIDE) * SIDE + y
                else:
                    source = x * SIDE + (y + distance) % SIDE
                pairs.append((source * 2 + core, (x * SIDE + y) * 2 + core))
    return lax.ppermute(value, ("x", "y", "c"), pairs)


def pack_kernel(parts, *refs):
    for i, source in enumerate(refs[:parts]):
        size = source.shape[0]
        for j, out_ref in enumerate(refs[parts:]):
            share = out_ref.shape[1]
            out_ref[pl.ds(i * size, size)] = source[:, j * share : (j + 1) * share]


def pack(parts, ends):
    size, genes, width = parts[0].shape
    shape = jax.ShapeDtypeStruct((len(parts) * size, genes // ends, width), parts[0].dtype)
    return pl.pallas_call(
        functools.partial(pack_kernel, len(parts)),
        out_shape=[shape] * ends,
        compiler_params=pltpu.CompilerParams(vmem_limit_bytes=16 * 1024 * 1024),
    )(*parts)


def line(value, ends):
    return pack([value] + [shift(value, d, 0) for d in (1, 2, 3)], ends)


def plane(value, ring):
    if not ring:
        return [value] + [shift(value, d, 1) for d in (1, 2, 3)]
    half = value.shape[0] // 2
    after, before = shift(value, 1, 1), shift(value, 3, 1)
    low, high = shift(after[:half], 1, 1), shift(before[half:], 3, 1)
    return [value, after, low, high, before]


def step_kernel(pieces, raw, ends, place_ref, count_ref, table_ref, *refs):
    sources, refs = refs[:pieces], refs[pieces:]
    if raw:
        inverse_ref, refs = refs[0], refs[1:]
    else:
        share_ref, refs = refs[0], refs[1:]
    aff_ref, out_refs, refs = refs[0], refs[1 : 1 + ends], refs[1 + ends :]
    peak_ref, refs = refs[0], refs[1:]
    if raw:
        own_peak_ref, refs = refs[0], refs[1:]
        share_ref, refs = refs[0], refs[1:]
    held, sems = refs
    blocks, slots = aff_ref.shape[:2]
    genes = held.shape[1]
    copies, start = [], 0
    for i, source in enumerate(sources):
        rows = source.shape[0]
        copies.append(pltpu.make_async_copy(source, held.at[pl.ds(start, rows)], sems.at[i]))
        start += rows
    for copy in copies:
        copy.start()
    for copy in copies:
        copy.wait()

    def fetch(item):
        tile = held[place_ref[item]]
        if raw:
            tile = tile.astype(jnp.float32) * inverse_ref[pl.ds(table_ref[item], 1), :]
            tile = tile.astype(jnp.bfloat16)
        return tile

    def one(row, peaks):
        count = count_ref[row]
        tiles = []
        for s in range(slots):
            tile = fetch(row * slots + s)
            if s == 0:
                own = tile.astype(jnp.float32)
            if raw:
                tile = jnp.concatenate([tile, jnp.ones((16, BS), tile.dtype)], axis=0)
            if s > REMOTE:
                tile = jnp.where(s < count, tile, jnp.zeros_like(tile))
            tiles.append(tile)
        left = jnp.concatenate(tiles, axis=1)
        right = aff_ref[row].reshape(slots * BS, BS)
        total = jnp.dot(left, right, preferred_element_type=jnp.float32)
        if raw:
            share_ref[pl.ds(row, 1)] = 0.5 / total[genes : genes + 1]
        mixed = 0.5 * own + total[:genes] * share_ref[pl.ds(row, 1)]
        for out_ref in out_refs:
            share = out_ref.shape[1]
            out_ref[row] = mixed[:share].astype(out_ref.dtype)
            mixed = jnp.concatenate([mixed[share:], mixed[:share]]) if ends > 1 else mixed
        found = (mixed, own) if raw else (mixed,)
        return tuple(jnp.maximum(a, b) for a, b in zip(peaks, found))

    def several(i, carry):
        for j in range(UNROLL):
            carry = one(i * UNROLL + j, carry)
        return carry

    carry = (jnp.zeros((genes, BS), jnp.float32),) * (1 + raw)
    carry = lax.fori_loop(0, blocks // UNROLL, several, carry)
    peak_ref[...] = carry[0]
    if raw:
        own_peak_ref[...] = carry[1]


def diffuse(pieces, places, counts, tables, inverse, share, affinity, ends):
    blocks = affinity.shape[0]
    genes = pieces[0].shape[1]
    total = sum(piece.shape[0] for piece in pieces)
    n = len(pieces)
    raw = inverse is not None
    smem = pl.BlockSpec(memory_space=pltpu.SMEM)
    vmem = pl.BlockSpec(memory_space=pltpu.VMEM)
    return pl.pallas_call(
        functools.partial(step_kernel, n, raw, ends),
        in_specs=[smem] * 3
        + [pl.BlockSpec(memory_space=pl.ANY)] * n
        + [vmem]
        + [vmem],
        out_specs=[vmem] * (ends + 1 + 2 * raw),
        scratch_shapes=[
            pltpu.VMEM((total, genes, BS), pieces[0].dtype),
            pltpu.SemaphoreType.DMA((n,)),
        ],
        out_shape=[jax.ShapeDtypeStruct((blocks, genes // ends, BS), jnp.bfloat16)] * ends
        + [jax.ShapeDtypeStruct((genes, BS), jnp.float32)] * (1 + raw)
        + [jax.ShapeDtypeStruct((blocks, BS), jnp.float32)] * raw,
        compiler_params=pltpu.CompilerParams(vmem_limit_bytes=32 * 1024 * 1024),
        cost_estimate=pl.CostEstimate(
            flops=2 * affinity.size * genes,
            bytes_accessed=2 * affinity.size,
            transcendentals=0,
        ),
    )(places, counts, tables, *pieces, inverse if raw else share, affinity)


def to_all(value, axis, size):
    return lax.all_to_all(
        jnp.broadcast_to(value[None], (size,) + value.shape), axis, 0, 0, tiled=True
    )


def local(stored, neighbours, counts, affinity):
    core, my_x, my_y = lax.axis_index("c"), lax.axis_index("x"), lax.axis_index("y")
    blocks_dev, slots = neighbours.shape
    part = lax.dynamic_slice_in_dim(affinity, core * (blocks_dev // 2), blocks_dev // 2, 0)
    affinity = lax.all_gather(part, ("z", "c"), tiled=True)

    genes_dev = stored.shape[0]
    cells_dev = blocks_dev * BS
    blocks = GROUP * blocks_dev
    counted = stored.reshape(genes_dev, GROUP, SIDE * SIDE, cells_dev)
    counted = lax.all_to_all(counted, XY, 2, 0, tiled=True)
    genes = counted.shape[0]
    counted = jnp.transpose(counted.reshape(genes, blocks, BS), (1, 0, 2))

    table = jnp.concatenate([neighbours, counts[:, None]], axis=1).reshape(1, -1)
    used = table.shape[1]
    table = jnp.pad(table.astype(jnp.float32), ((0, 7), (0, BS - used)))
    sums = jnp.sum(counted.astype(jnp.float32), axis=1)
    sums = sums + lax.ppermute(sums, "c", [(0, 1), (1, 0)])
    sums = to_all(jnp.concatenate([sums, table]), "z", GROUP)
    inverse = (2 * GROUP * genes) / jnp.sum(sums[:, :blocks], axis=0)
    inverse = to_all(inverse, XY, SIDE * SIDE).reshape(-1, BS)
    table = sums[:, blocks, :used].astype(jnp.int32).reshape(blocks, slots + 1)
    neighbours, counts = table[:, :slots], table[:, slots]

    device, inner = neighbours // blocks_dev, neighbours % blocks_dev
    within = device // (SIDE * SIDE) * blocks_dev + inner
    dx = (device // SIDE - my_x) % SIDE
    dy = (device - my_y) % SIDE
    first, second = jnp.where(core == 0, dx, dy), jnp.where(core == 0, dy, dx)
    places = ((second * SIDE + first) * blocks + within).reshape(-1)
    tables = ((device % (SIDE * SIDE)) * blocks + within).reshape(-1)

    current, peak, own_peak, share = diffuse(
        plane(*line(counted, 1), False), places, counts, tables, inverse, None, affinity, 1
    )
    peaks = [own_peak, peak]
    lines = line(current, STREAMS)
    for step in range(1, STEPS):
        if step > 1:
            lines = [line(stream, 1)[0] for stream in streams]
        ends = [
            diffuse(plane(part, True), places, counts, tables, None, share, affinity, 1) for part in lines
        ]
        streams = [end[0] for end in ends]
        peaks.append(jnp.concatenate([end[1] for end in ends]))
    current = jnp.concatenate(streams, axis=1)
    peaks = jnp.max(jnp.stack(peaks), axis=2).reshape(-1)
    peaks = jnp.max(to_all(peaks, XY, SIDE * SIDE), axis=0).reshape(STEPS + 1, genes)
    scale = jnp.ones((genes,), jnp.float32)
    for step in range(STEPS):
        scale = scale * (peaks[0] / (scale * peaks[1 + step] + epsilon))
    result = (current.astype(jnp.float32) * scale[None, :, None]).astype(jnp.bfloat16)
    result = lax.all_to_all(result, "z", 0, 0, tiled=True)
    result = result.reshape(GROUP, blocks_dev, genes, BS).astype(jnp.float32)
    return jnp.transpose(result, (0, 2, 1, 3)).reshape(GROUP * genes, cells_dev)


def solution(mesh):
    grid = Mesh(mesh.devices.reshape(GROUP, SIDE, SIDE, 2), ("z", "x", "y", "c"))
    cells = ("z", "x", "y")
    return jax.shard_map(
        local,
        mesh=grid,
        in_specs=(P(cells, "c", None), P(cells, None), P(cells), P(cells, None, None, None)),
        out_specs=P("c", cells),
        check_vma=False,
    )
```

```python
import functools

import jax
import jax.numpy as jnp
from jax import lax
from jax.experimental import pallas as pl
from jax.experimental.pallas import tpu as pltpu
from jax.sharding import Mesh, PartitionSpec as P

REMOTE = 4
STEPS = 3
SIDE = 4
GROUP = 8
BS = 128
STREAMS = 2
UNROLL = 16
epsilon = 1e-06
XY = ("x", "y")


def shift(value, distance, stage):
    pairs = []
    for x in range(SIDE):
        for y in range(SIDE):
            for core in range(2):
                if core == stage:
                    source = ((x + distance) % SIDE) * SIDE + y
                else:
                    source = x * SIDE + (y + distance) % SIDE
                pairs.append((source * 2 + core, (x * SIDE + y) * 2 + core))
    return lax.ppermute(value, ("x", "y", "c"), pairs)


def pack_kernel(parts, *refs):
    for i, source in enumerate(refs[:parts]):
        size = source.shape[0]
        for j, out_ref in enumerate(refs[parts:]):
            share = out_ref.shape[1]
            out_ref[pl.ds(i * size, size)] = source[:, j * share : (j + 1) * share]


def pack(parts, ends):
    size, genes, width = parts[0].shape
    shape = jax.ShapeDtypeStruct((len(parts) * size, genes // ends, width), parts[0].dtype)
    return pl.pallas_call(
        functools.partial(pack_kernel, len(parts)),
        out_shape=[shape] * ends,
        compiler_params=pltpu.CompilerParams(vmem_limit_bytes=16 * 1024 * 1024),
    )(*parts)


def line(value, ends):
    return pack([value] + [shift(value, d, 0) for d in (1, 2, 3)], ends)


def plane(value, ring):
    if not ring:
        return [value] + [shift(value, d, 1) for d in (1, 2, 3)]
    half = value.shape[0] // 2
    after, before = shift(value, 1, 1), shift(value, 3, 1)
    low, high = shift(after[:half], 1, 1), shift(before[half:], 3, 1)
    return [value, after, low, high, before]


def step_kernel(pieces, raw, ends, place_ref, count_ref, table_ref, *refs):
    sources, refs = refs[:pieces], refs[pieces:]
    if raw:
        inverse_ref, refs = refs[0], refs[1:]
    else:
        share_ref, refs = refs[0], refs[1:]
    aff_ref, out_refs, refs = refs[0], refs[1 : 1 + ends], refs[1 + ends :]
    peak_ref, refs = refs[0], refs[1:]
    if raw:
        own_peak_ref, refs = refs[0], refs[1:]
        share_ref, refs = refs[0], refs[1:]
    held, sems = refs
    blocks, slots = aff_ref.shape[:2]
    genes = held.shape[1]
    copies, start = [], 0
    for i, source in enumerate(sources):
        rows = source.shape[0]
        copies.append(pltpu.make_async_copy(source, held.at[pl.ds(start, rows)], sems.at[i]))
        start += rows
    for copy in copies:
        copy.start()
    for copy in copies:
        copy.wait()

    def fetch(item):
        tile = held[place_ref[item]]
        if raw:
            tile = tile.astype(jnp.float32) * inverse_ref[pl.ds(table_ref[item], 1), :]
            tile = tile.astype(jnp.bfloat16)
        return tile

    def one(row, peaks):
        count = count_ref[row]
        tiles = []
        for s in range(slots):
            tile = fetch(row * slots + s)
            if s == 0:
                own = tile.astype(jnp.float32)
            if raw:
                tile = jnp.concatenate([tile, jnp.ones((16, BS), tile.dtype)], axis=0)
            if s > REMOTE:
                tile = jnp.where(s < count, tile, jnp.zeros_like(tile))
            tiles.append(tile)
        left = jnp.concatenate(tiles, axis=1)
        right = aff_ref[row].reshape(slots * BS, BS)
        total = jnp.dot(left, right, preferred_element_type=jnp.float32)
        if raw:
            share_ref[pl.ds(row, 1)] = 0.5 / total[genes : genes + 1]
        mixed = 0.5 * own + total[:genes] * share_ref[pl.ds(row, 1)]
        for out_ref in out_refs:
            share = out_ref.shape[1]
            out_ref[row] = mixed[:share].astype(out_ref.dtype)
            mixed = jnp.concatenate([mixed[share:], mixed[:share]]) if ends > 1 else mixed
        found = (mixed, own) if raw else (mixed,)
        return tuple(jnp.maximum(a, b) for a, b in zip(peaks, found))

    def several(i, carry):
        for j in range(UNROLL):
            carry = one(i * UNROLL + j, carry)
        return carry

    carry = (jnp.zeros((genes, BS), jnp.float32),) * (1 + raw)
    carry = lax.fori_loop(0, blocks // UNROLL, several, carry)
    peak_ref[...] = carry[0]
    if raw:
        own_peak_ref[...] = carry[1]


def diffuse(pieces, places, counts, tables, inverse, share, affinity, ends):
    blocks = affinity.shape[0]
    genes = pieces[0].shape[1]
    total = sum(piece.shape[0] for piece in pieces)
    n = len(pieces)
    raw = inverse is not None
    smem = pl.BlockSpec(memory_space=pltpu.SMEM)
    vmem = pl.BlockSpec(memory_space=pltpu.VMEM)
    return pl.pallas_call(
        functools.partial(step_kernel, n, raw, ends),
        in_specs=[smem] * 3
        + [pl.BlockSpec(memory_space=pl.ANY)] * n
        + [vmem]
        + [vmem],
        out_specs=[vmem] * (ends + 1 + 2 * raw),
        scratch_shapes=[
            pltpu.VMEM((total, genes, BS), pieces[0].dtype),
            pltpu.SemaphoreType.DMA((n,)),
        ],
        out_shape=[jax.ShapeDtypeStruct((blocks, genes // ends, BS), jnp.bfloat16)] * ends
        + [jax.ShapeDtypeStruct((genes, BS), jnp.float32)] * (1 + raw)
        + [jax.ShapeDtypeStruct((blocks, BS), jnp.float32)] * raw,
        compiler_params=pltpu.CompilerParams(vmem_limit_bytes=32 * 1024 * 1024),
        cost_estimate=pl.CostEstimate(
            flops=2 * affinity.size * genes,
            bytes_accessed=2 * affinity.size,
            transcendentals=0,
        ),
    )(places, counts, tables, *pieces, inverse if raw else share, affinity)


def to_all(value, axis, size):
    return lax.all_to_all(
        jnp.broadcast_to(value[None], (size,) + value.shape), axis, 0, 0, tiled=True
    )


def local(stored, neighbours, counts, affinity):
    core, my_x, my_y = lax.axis_index("c"), lax.axis_index("x"), lax.axis_index("y")
    blocks_dev, slots = neighbours.shape
    half = blocks_dev // 2
    part = jnp.where(core == 0, affinity[:half], affinity[half:])
    affinity = lax.all_gather(part, ("z", "c"), tiled=True)

    genes_dev = stored.shape[0]
    cells_dev = blocks_dev * BS
    blocks = GROUP * blocks_dev
    counted = stored.reshape(genes_dev, GROUP, SIDE * SIDE, cells_dev)
    counted = lax.all_to_all(counted, XY, 2, 0, tiled=True)
    genes = counted.shape[0]
    counted = jnp.transpose(counted.reshape(genes, blocks, BS), (1, 0, 2))

    table = jnp.concatenate([neighbours, counts[:, None]], axis=1).reshape(1, -1)
    used = table.shape[1]
    table = jnp.pad(table.astype(jnp.float32), ((0, 7), (0, BS - used)))
    sums = jnp.sum(counted.astype(jnp.float32), axis=1)
    sums = sums + lax.ppermute(sums, "c", [(0, 1), (1, 0)])
    sums = to_all(jnp.concatenate([sums, table]), "z", GROUP)
    inverse = (2 * GROUP * genes) / jnp.sum(sums[:, :blocks], axis=0)
    inverse = to_all(inverse, XY, SIDE * SIDE).reshape(-1, BS)
    table = sums[:, blocks, :used].astype(jnp.int32).reshape(blocks, slots + 1)
    neighbours, counts = table[:, :slots], table[:, slots]

    device, inner = neighbours // blocks_dev, neighbours % blocks_dev
    within = device // (SIDE * SIDE) * blocks_dev + inner
    dx = (device // SIDE - my_x) % SIDE
    dy = (device - my_y) % SIDE
    first, second = jnp.where(core == 0, dx, dy), jnp.where(core == 0, dy, dx)
    places = ((second * SIDE + first) * blocks + within).reshape(-1)
    tables = ((device % (SIDE * SIDE)) * blocks + within).reshape(-1)

    current, peak, own_peak, share = diffuse(
        plane(*line(counted, 1), False), places, counts, tables, inverse, None, affinity, 1
    )
    peaks = [own_peak, peak]
    lines = line(current, STREAMS)
    for step in range(1, STEPS):
        if step > 1:
            lines = [line(stream, 1)[0] for stream in streams]
        ends = [
            diffuse(plane(part, True), places, counts, tables, None, share, affinity, 1) for part in lines
        ]
        streams = [end[0] for end in ends]
        peaks.append(jnp.concatenate([end[1] for end in ends]))
    current = jnp.concatenate(streams, axis=1)
    peaks = jnp.max(jnp.stack(peaks), axis=2).reshape(-1)
    peaks = jnp.max(to_all(peaks, XY, SIDE * SIDE), axis=0).reshape(STEPS + 1, genes)
    scale = jnp.ones((genes,), jnp.float32)
    for step in range(STEPS):
        scale = scale * (peaks[0] / (scale * peaks[1 + step] + epsilon))
    result = (current.astype(jnp.float32) * scale[None, :, None]).astype(jnp.bfloat16)
    result = lax.all_to_all(result, "z", 0, 0, tiled=True)
    result = result.reshape(GROUP, blocks_dev, genes, BS).astype(jnp.float32)
    return jnp.transpose(result, (0, 2, 1, 3)).reshape(GROUP * genes, cells_dev)


def solution(mesh):
    grid = Mesh(mesh.devices.reshape(GROUP, SIDE, SIDE, 2), ("z", "x", "y", "c"))
    cells = ("z", "x", "y")
    return jax.shard_map(
        local,
        mesh=grid,
        in_specs=(P(cells, "c", None), P(cells, None), P(cells), P(cells, None, None, None)),
        out_specs=P("c", cells),
        check_vma=False,
    )
```
